32 devices in a mesh: row: 4 (over y, x), col: 2 (over core), layer: 4 (over z).
Axes of the slice: x: 2, y: 2, z: 4, core: 2. Of those that a mesh axis runs over, the one named last changes fastest.
Arguments:
- density: bfloat16 [8192, 8192], P('row', 'col'), may hold values from -0.59765625 to 0.59765625
- density_pattern: int32 [64, 64], replicated, may hold values from 0 to 1, as said below
- result_pattern: int32 [64, 64], replicated, may hold values from 0 to 1, as said below
Outputs:
- purified: bfloat16 [8192, 4, 2048], P('row', 'layer', 'col')
The draws below stay inside these ranges and needn't reach their ends.
Inputs may be any that keep to these rules, and one draw needn't show every extreme that they name: `density_pattern`: symmetric, with ones on the diagonal; blocks are atom clusters in a periodic chain, and a block row keeps the blocks within a cutoff distance of its cluster that varies from row to row. `result_pattern`: symmetric; keeps the blocks within a somewhat larger cutoff distance than density_pattern.
All inputs are finite; a program needn't handle non-finite values.
Results may differ from the reference program's by a relative error of at most 0.017.
Values may be sent and summed in bfloat16 or wider, within the bound.
No kernel may reach another device: no remote copies, remote signals or barrier semaphores. Data moves between devices by JAX's collectives and lax.ppermute only.
A program may use at most 128 MiB of HBM per device.

```python
import jax
import jax.numpy as jnp

B = 128
NB = 64
M = 8192
N_LAYER = 4


def cluster_layout(key):
    radius = jax.random.randint(jax.random.fold_in(key, 17), (NB,), NB // 16, NB // 2 + 1)
    radius = radius.at[0].set(NB // 2).at[NB // 2].set(NB // 2)
    positions = jnp.arange(NB, dtype=jnp.int32)
    apart = jnp.abs(positions[:, None] - positions[None, :])
    apart = jnp.minimum(apart, NB - apart)
    reach = (radius[:, None] + radius[None, :]) // 2
    return (apart, reach)


def draw_density_pattern(key, part):
    apart, reach = cluster_layout(key)
    return (apart <= reach).astype(jnp.int32)


def draw_result_pattern(key, part):
    apart, reach = cluster_layout(key)
    return (apart <= reach + 8).astype(jnp.int32)


def block_levels(stream_key, extent, cuts, smallest, top_value):
    level = 1.0
    for axis_at, shards_of in cuts:
        steps = jax.random.uniform(jax.random.fold_in(jax.random.fold_in(stream_key, 6), axis_at), (shards_of,), jnp.float32, smallest / len(cuts), top_value / len(cuts))
        level = level * jnp.repeat(jnp.exp(steps), extent[axis_at] // shards_of).reshape((-1,) + (1,) * (len(extent) - 1 - axis_at))
    return level


def gaussian(rng, dims, spread, limit, shards=(), kind=jnp.bfloat16):
    result = jax.random.normal(rng, dims, jnp.float32) * spread
    if len(shards) > 0:
        result = block_levels(rng, dims, shards, -0.22, 0.18) * result
    return jnp.clip(result, min=-limit, max=limit).astype(kind)


def setup_inputs(seed: int = 0) -> dict:
    key_of = jax.random.split(jax.random.key(seed), 4)
    return {
        "density": gaussian(key_of[0], (M, M), 0.1, 0.59765625, ((0, 4), (1, 2))),
        "density_pattern": draw_density_pattern(jax.random.fold_in(key_of[3], 71), 0),
        "result_pattern": draw_result_pattern(jax.random.fold_in(key_of[3], 71), 0),
    }


def expand_blocks(pattern):
    return jnp.repeat(jnp.repeat(pattern, B, axis=0), B, axis=1)


def reference(density, density_pattern, result_pattern):
    masked = density * expand_blocks(density_pattern).astype(jnp.bfloat16)
    square = jnp.dot(masked, masked, preferred_element_type=jnp.float32)
    square_rounded = square.astype(jnp.bfloat16)
    cube = jnp.dot(square_rounded, masked, preferred_element_type=jnp.float32)
    combined = (3.0 * square - 2.0 * cube) * expand_blocks(result_pattern).astype(jnp.float32)
    order = NB * B
    grouped = combined.reshape(order, NB // N_LAYER, N_LAYER, B).transpose(0, 2, 1, 3)
    return grouped.reshape(order, N_LAYER, NB // N_LAYER * B).astype(jnp.bfloat16)
```

```python
import functools

import jax
import jax.numpy as jnp
from jax import lax
from jax.experimental import pallas as pl
from jax.experimental.pallas import tpu as pltpu
from jax.sharding import PartitionSpec as P

B = 128
STEP = 4
TILE = 2
VMEM = 56 * 2**20


def swap(x, axis, distance):
    size = lax.axis_size(axis)
    return lax.ppermute(x, axis, [(i, i ^ distance) for i in range(size)])


def after(x, *earlier):
    return lax.optimization_barrier((x, *earlier))[0]


def exchange(own, gate):
    half = own.shape[0] // 2
    if gate is not None:
        own = after(own, *gate)
    across = swap(own, "row", 1)
    along = swap(own, "row", 2)
    far_top = swap(across[:half], "row", 2)
    far_bottom = swap(along[half:], "row", 1)
    return across, along, far_top, far_bottom


def pick_kernel(start, where, keep, x_ref, o_ref):
    q = pl.program_id(0)
    for i in range(x_ref.shape[0] // B):
        rows = pl.ds(i * B, B)
        kept = keep[i, start + q] != 0
        o_ref[rows, :] = jnp.where(kept, x_ref[rows, :], jnp.zeros((B, B), o_ref.dtype))


def pick_columns(density, keep, layer, layers, start, group):
    rows = density.shape[0]
    return pl.pallas_call(
        functools.partial(pick_kernel, start),
        grid_spec=pltpu.PrefetchScalarGridSpec(
            num_scalar_prefetch=2,
            grid=(group,),
            in_specs=[pl.BlockSpec((rows, B), lambda q, where, keep: (0, (start + q) * layers + where[0]))],
            out_specs=pl.BlockSpec((rows, B), lambda q, where, keep: (0, q)),
        ),
        out_shape=jax.ShapeDtypeStruct((rows, group * B), density.dtype),
        compiler_params=pltpu.CompilerParams(vmem_limit_bytes=VMEM),
        name="pick_columns",
    )(jnp.reshape(layer, (1,)), keep, density)


def product_kernel(plan, n_src, splits, first, last, column, meta, active, keep, *refs):
    refs = list(refs)
    take = lambda n: [refs.pop(0) for _ in range(n)]
    n_part = len(plan)
    lhs = [take(n_src) for _ in range(n_part)]
    masks = take(n_part)
    panels = [take(n) for n in splits]
    total_in = None if first else take(1)[0]
    square_in = take(1)[0] if last else None
    if last and column > 0:
        take(1)
    outs = refs[:-1]
    total = refs[-1]
    i = pl.program_id(0)
    tile = total.shape[0]
    total[...] = jnp.zeros_like(total) if first else total_in[...]
    for p, m in enumerate(plan):
        source, owner = meta[3 * m], meta[3 * m + 2]
        depth = lhs[p][0].shape[1]
        steps = depth // (STEP * B)
        piece = depth // splits[p]
        for s in range(steps):
            cols = pl.ds(s * STEP * B, STEP * B)
            at = s * STEP * B
            panel = panels[p][at // piece]
            used = active[i, owner * steps + s] != 0
            for h in range(n_src):
                @pl.when(used & (source == h) if n_src > 1 else used)
                def _():
                    kept = [
                        jnp.broadcast_to(masks[p][0, t:t + 1, cols], (B, STEP * B))
                        for t in range(tile // B)
                    ]
                    kept = jnp.concatenate(kept, axis=0).astype(jnp.bfloat16)
                    total[...] += jnp.dot(
                        lhs[p][h][:, cols] * kept,
                        panel[pl.ds(at % piece, STEP * B), :],
                        preferred_element_type=jnp.float32,
                    )
    if not last:
        outs[0][...] = total[...]
        if len(outs) > 1:
            outs[1][...] = total[...].astype(outs[1].dtype)
        return
    step = total.shape[1] // B
    for t in range(tile // B):
        for q in range(step):
            at = (pl.ds(t * B, B), pl.ds(q * B, B))
            value = 3.0 * square_in[at] - 2.0 * total[at]
            kept = keep[i * (tile // B) + t, column * step + q] != 0
            outs[0][at] = jnp.where(kept, value, 0.0).astype(outs[0].dtype)


def product(plan, meta, active, keep, sources, mask, panels, total=None, rounded=False,
            square=None, out=None, column=0):
    rows = sources[0].shape[0]
    width = panels[0][0].shape[1]
    tile = TILE * B
    n_src = len(sources)
    depth = rows
    first, last = total is None, square is not None
    specs, args = [], []
    for m in plan:
        for h in range(n_src):
            def index(i, meta, active, keep, m=m, h=h):
                here = meta[3 * m] == h
                return jnp.where(here, i, 0), jnp.where(here, meta[3 * m + 1], 0)
            specs.append(pl.BlockSpec((tile, depth), index))
            args.append(sources[h])
    for m in plan:
        specs.append(pl.BlockSpec((1, TILE, depth), lambda i, meta, active, keep, m=m: (i, 0, meta[3 * m + 2])))
        args.append(mask)
    for group in panels:
        for panel in group:
            specs.append(pl.BlockSpec(panel.shape, lambda i, *_: (0, 0), pipeline_mode=pl.Buffered(1)))
            args.append(panel)
    row_block = pl.BlockSpec((tile, width), lambda i, *_: (i, 0))
    if not first:
        specs.append(row_block)
        args.append(total)
    aliases = {}
    if last:
        specs.append(row_block)
        args.append(square)
        if column > 0:
            specs.append(pl.BlockSpec(memory_space=pl.ANY))
            args.append(out)
            aliases = {3 + len(args) - 1: 0}
        out_shape = [jax.ShapeDtypeStruct(out if column == 0 else out.shape, jnp.bfloat16)]
        out_specs = [pl.BlockSpec((tile, width), lambda i, *_: (i, column))]
    else:
        out_shape = [jax.ShapeDtypeStruct((rows, width), jnp.float32)]
        out_specs = [row_block]
        if rounded:
            out_shape.append(jax.ShapeDtypeStruct((rows, width), jnp.bfloat16))
            out_specs.append(row_block)
    flops = 2 * rows * depth * len(plan) * width
    result = pl.pallas_call(
        functools.partial(product_kernel, plan, n_src, [len(g) for g in panels], first, last, column),
        grid_spec=pltpu.PrefetchScalarGridSpec(
            num_scalar_prefetch=3,
            grid=(rows // tile,),
            in_specs=specs,
            out_specs=out_specs,
            scratch_shapes=[pltpu.VMEM((tile, width), jnp.float32)],
        ),
        out_shape=out_shape,
        input_output_aliases=aliases,
        cost_estimate=pl.CostEstimate(
            flops=flops, bytes_accessed=2 * rows * depth * len(plan), transcendentals=0),
        compiler_params=pltpu.CompilerParams(vmem_limit_bytes=VMEM),
        name="product",
    )(meta, active, keep, *args)
    return result if rounded else result[0]


def shards(density, density_pattern, result_pattern):
    rows, cols = density.shape
    layers = lax.axis_size("layer")
    n_col = lax.axis_size("col")
    block_rows, block_cols = rows // B, cols // B
    group = block_cols // layers
    width = group * B
    r, c, l = (lax.axis_index(a) for a in ("row", "col", "layer"))
    n_chunk = 2 if group % 4 == 0 else 1
    chunk_w = width // n_chunk

    def pattern_tile(pattern):
        here = lax.dynamic_slice(pattern, (r * block_rows, c * block_cols), (block_rows, block_cols))
        return lax.dynamic_index_in_dim(here.reshape(block_rows, group, layers), l, 2, keepdims=False)

    if n_col == 2:
        sources = [density, swap(density, "col", 1)]
    else:
        sources = [lax.all_gather(density, "col", axis=1, tiled=True)]
    own_mask = pattern_tile(density_pattern)
    step = group // n_chunk
    own_chunks = [
        pick_columns(density, own_mask, l, layers, j * step, step) for j in range(n_chunk)
    ]
    row_mask = lax.dynamic_slice_in_dim(density_pattern, r * block_rows, block_rows, 0)
    n_block = row_mask.shape[1]
    active = row_mask.reshape(block_rows // TILE, TILE, n_block // STEP, STEP).max(axis=(1, 3))
    mask = jnp.repeat(row_mask.astype(jnp.float32), B, axis=1)
    mask = mask.reshape(block_rows // TILE, TILE, n_block * B)
    keep = pattern_tile(result_pattern)
    meta = []
    per_source = n_block * B // rows // len(sources)
    for m in range(4):
        owner = r ^ m
        source = (owner // per_source != c) if len(sources) == 2 else 0
        meta += [source, owner % per_source, owner]
    meta = jnp.stack([jnp.asarray(v, jnp.int32) for v in meta])
    run = functools.partial(product, meta=meta, active=active, keep=keep, sources=sources, mask=mask)

    gate = None
    density_panels = []
    for j in range(n_chunk):
        panels = exchange(own_chunks[j], gate)
        gate = panels[:2]
        density_panels.append(panels)
    squares, rounded = [], []
    for j in range(n_chunk):
        across, along, top, bottom = density_panels[j]
        total, low = run([0, 1, 2, 3], panels=[[own_chunks[j]], [across], [along], [top, bottom]], rounded=True)
        squares.append(total)
        rounded.append(low)
    square_panels = []
    for j in range(n_chunk):
        panels = exchange(rounded[j], gate)
        gate = panels[:2]
        square_panels.append(panels)
    out = (rows, width)
    for j in range(n_chunk):
        across, along, top, bottom = square_panels[j]
        total = run([0, 1, 2], panels=[[rounded[j]], [across], [along]])
        out = run([3], panels=[[top, bottom]], total=total, square=squares[j], out=out, column=j)
    return out.reshape(rows, 1, width)


def solution(mesh):
    return jax.shard_map(
        shards,
        mesh=mesh,
        in_specs=(P("row", "col"), P(), P()),
        out_specs=P("row", "layer", "col"),
        check_vma=False,
    )
```

```python
import functools

import jax
import jax.numpy as jnp
from jax import lax
from jax.experimental import pallas as pl
from jax.experimental.pallas import tpu as pltpu
from jax.sharding import PartitionSpec as P

B = 128
TILE = 2
VMEM = 56 * 2**20


def swap(x, axis, distance):
    size = lax.axis_size(axis)
    return lax.ppermute(x, axis, [(i, i ^ distance) for i in range(size)])


def after(x, *earlier):
    return lax.optimization_barrier((x, *earlier))[0]


class Exchange:
    def __init__(self, own, whole, *gate):
        self.own, self.whole = own, whole
        if gate:
            own = after(own, *gate)
        half = own.shape[0] // 2
        self.top, self.bottom = own[:half], own[half:]
        if whole:
            self.across, self.along = [swap(own, "row", 1)], [swap(own, "row", 2)]
            self.hops = self.across[0][:half], self.along[0][half:]
        else:
            self.hops = swap(self.top, "row", 1), swap(self.bottom, "row", 2)

    def second(self, *gate):
        if not self.whole:
            top, bottom = after(self.top, *gate), after(self.bottom, *gate)
            self.across = [self.hops[0], swap(bottom, "row", 1)]
            self.along = [swap(top, "row", 2), self.hops[1]]

    def relay(self, *gate):
        top, bottom = (after(x, *gate) if gate else x for x in self.hops)
        self.far = [swap(top, "row", 2), swap(bottom, "row", 1)]

    def near(self):
        return [[self.own], self.across, self.along]


def pick_kernel(start, where, keep, x_ref, o_ref):
    q = pl.program_id(0)
    for i in range(x_ref.shape[0] // B):
        kept = keep[i, start + q] != 0
        rows = pl.ds(i * B, B)
        block = x_ref[rows, :]
        o_ref[rows, :] = jnp.where(kept, block, jnp.zeros_like(block))


def pick_columns(density, keep, layer, layers, start, group):
    rows = density.shape[0]
    return pl.pallas_call(
        functools.partial(pick_kernel, start),
        grid_spec=pltpu.PrefetchScalarGridSpec(
            num_scalar_prefetch=2,
            grid=(group,),
            in_specs=[
                pl.BlockSpec((rows, B), lambda q, where, keep: (0, (start + q) * layers + where[0]))
            ],
            out_specs=pl.BlockSpec((rows, B), lambda q, where, keep: (0, q)),
        ),
        out_shape=jax.ShapeDtypeStruct((rows, group * B), density.dtype),
        compiler_params=pltpu.CompilerParams(vmem_limit_bytes=VMEM),
        name="pick_columns",
    )(jnp.reshape(layer, (1,)), keep, density)


def product_kernel(plan, pieces, full, first, last, column, meta, keep, *refs):
    refs = list(refs)
    take = lambda n: [refs.pop(0) for _ in range(n)]
    n_slot = meta.shape[0] // 3
    lhs, masks = take(n_slot), take(n_slot)
    panels = [take(n) for n in pieces]
    total_in = None if first else take(1)[0]
    square_in = take(1)[0] if last else None
    if last and column > 0:
        take(1)
    total, held, sems = refs[-3:]
    outs = refs[:-3]
    i = pl.program_id(0)
    tile = total.shape[0]
    depth = held.shape[0] // n_slot

    @pl.when(i == 0)
    def _():
        copies = []
        for p, m in enumerate(plan):
            for h, panel in enumerate(panels[p]):
                size = panel.shape[0]
                at = pl.multiple_of(meta[m] * depth + h * size, size)
                copies.append(pltpu.make_async_copy(
                    panel, held.at[pl.ds(at, size)], sems.at[len(copies)]))
        for copy in copies:
            copy.start()
        for copy in copies:
            copy.wait()

    total[...] = jnp.zeros_like(total) if first else total_in[...]
    for s in range(n_slot):
        def add():
            kept = [
                jnp.broadcast_to(masks[s][0, t:t + 1, :], (B, depth)) for t in range(tile // B)
            ]
            kept = jnp.concatenate(kept, axis=0).astype(jnp.bfloat16)
            total[...] += jnp.dot(
                lhs[s][...] * kept, held[pl.ds(s * depth, depth), :],
                preferred_element_type=jnp.float32)

        if full:
            add()
        else:
            pl.when(meta[2 * n_slot + s] != 0)(add)
    if not last:
        outs[0][...] = total[...]
        if len(outs) > 1:
            outs[1][...] = total[...].astype(jnp.bfloat16)
        return
    step = total.shape[1] // B
    for t in range(tile // B):
        for q in range(step):
            at = (pl.ds(t * B, B), pl.ds(q * B, B))
            value = 3.0 * square_in[at] - 2.0 * total[at]
            kept = keep[i * (tile // B) + t, column * step + q] != 0
            outs[0][at] = jnp.where(kept, value, 0.0).astype(outs[0].dtype)


def product(plan, slots, owners, keep, sources, mask, panels, total=None, rounded=False,
            square=None, out=None, column=0):
    rows = sources[0].shape[0]
    width = panels[0][0].shape[1]
    tile = TILE * B
    depth = rows
    steps = rows // tile
    n_slot = len(slots)
    per_source = n_slot // len(sources)
    first, last, full = total is None, square is not None, len(plan) == n_slot
    used = [sum((slots[m] == s).astype(jnp.int32) for m in plan) for s in range(n_slot)]
    meta = jnp.stack([*slots, *owners, *used])
    pieces = [len(group) for group in panels]
    specs, args = [], []
    for s in range(n_slot):
        def index(i, meta, keep, s=s):
            return i if full else jnp.where(meta[2 * n_slot + s] != 0, i, 0), s % per_source
        specs.append(pl.BlockSpec((tile, depth), index))
        args.append(sources[s // per_source])
    for s in range(n_slot):
        specs.append(
            pl.BlockSpec((1, TILE, depth), lambda i, meta, keep, s=s: (i, 0, meta[n_slot + s])))
        args.append(mask)
    for group in panels:
        for panel in group:
            specs.append(pl.BlockSpec(memory_space=pl.ANY))
            args.append(panel)
    row_block = pl.BlockSpec((tile, width), lambda i, *_: (i, 0))
    if not first:
        specs.append(row_block)
        args.append(total)
    aliases = {}
    if last:
        specs.append(row_block)
        args.append(square)
        if column > 0:
            specs.append(pl.BlockSpec(memory_space=pl.ANY))
            args.append(out)
            aliases = {2 + len(args) - 1: 0}
        out_shape = [jax.ShapeDtypeStruct(out if column == 0 else out.shape, jnp.bfloat16)]
        out_specs = [pl.BlockSpec((tile, width), lambda i, *_: (i, column))]
    else:
        out_shape = [jax.ShapeDtypeStruct((rows, width), jnp.float32)]
        out_specs = [row_block]
        if rounded:
            out_shape.append(jax.ShapeDtypeStruct((rows, width), jnp.bfloat16))
            out_specs.append(row_block)
    flops = 2 * rows * depth * len(plan) * width
    result = pl.pallas_call(
        functools.partial(product_kernel, plan, pieces, full, first, last, column),
        grid_spec=pltpu.PrefetchScalarGridSpec(
            num_scalar_prefetch=2,
            grid=(steps,),
            in_specs=specs,
            out_specs=out_specs,
            scratch_shapes=[
                pltpu.VMEM((tile, width), jnp.float32),
                pltpu.VMEM((n_slot * depth, width), jnp.bfloat16),
                pltpu.SemaphoreType.DMA((sum(pieces),)),
            ],
        ),
        out_shape=out_shape,
        input_output_aliases=aliases,
        cost_estimate=pl.CostEstimate(
            flops=flops, bytes_accessed=2 * rows * depth * len(plan), transcendentals=0),
        compiler_params=pltpu.CompilerParams(vmem_limit_bytes=VMEM),
        name="product",
    )(meta, keep, *args)
    return result if rounded else result[0]


def shards(density, density_pattern, result_pattern):
    rows, cols = density.shape
    layers = lax.axis_size("layer")
    n_col = lax.axis_size("col")
    block_rows, block_cols = rows // B, cols // B
    group = block_cols // layers
    width = group * B
    r, c, l = (lax.axis_index(a) for a in ("row", "col", "layer"))
    n_chunk = 2 if group % 4 == 0 else 1
    chunk_w = width // n_chunk

    def pattern_tile(pattern):
        here = lax.dynamic_slice(pattern, (r * block_rows, c * block_cols), (block_rows, block_cols))
        return lax.dynamic_index_in_dim(here.reshape(block_rows, group, layers), l, 2, keepdims=False)

    if n_col == 2:
        sources = [density, swap(density, "col", 1)]
    else:
        sources = [lax.all_gather(density, "col", axis=1, tiled=True)]
    own_mask = pattern_tile(density_pattern)
    step = group // n_chunk
    own_chunks = [
        pick_columns(density, own_mask, l, layers, j * step, step) for j in range(n_chunk)
    ]
    row_mask = lax.dynamic_slice_in_dim(density_pattern, r * block_rows, block_rows, 0)
    n_block = row_mask.shape[1]
    mask = jnp.repeat(row_mask.astype(jnp.float32), B, axis=1)
    mask = mask.reshape(block_rows // TILE, TILE, n_block * B)
    keep = pattern_tile(result_pattern)
    n_slot = n_block * B // rows
    per_source = n_slot // len(sources)
    slots, owners = [], []
    for m in range(n_slot):
        owner = r ^ m
        source = (owner // per_source != c).astype(jnp.int32) if len(sources) == 2 else 0
        slots.append(source * per_source + owner % per_source)
        source = m // per_source
        owners.append((c ^ source) * per_source + m % per_source if len(sources) == 2 else jnp.int32(m))
    run = functools.partial(
        product, slots=slots, owners=owners, keep=keep, sources=sources, mask=mask)

    every = list(range(n_slot))
    near, far = every[:-1], every[-1:]

    def exchange(own, *early):
        first = Exchange(own[0], True)
        rest = [Exchange(x, False, *early) for x in own[1:]]
        first.relay(*early)
        total = run(near, panels=first.near())
        for x in rest:
            x.second(total)
            x.relay()
        return [first, *rest], total

    (first, *rest), total = exchange(own_chunks, *sources[1:])
    sums = [run(far, panels=[first.far], total=total, rounded=True)]
    sums += [run(every, panels=[*x.near(), x.far], rounded=True) for x in rest]
    (first, *rest), total = exchange([low for _, low in sums])
    totals = [total, *(run(near, panels=x.near()) for x in rest)]
    out = (rows, width)
    for j, x in enumerate([first, *rest]):
        out = run(far, panels=[x.far], total=totals[j], square=sums[j][0], out=out, column=j)
    return out.reshape(rows, 1, width)


def solution(mesh):
    return jax.shard_map(
        shards,
        mesh=mesh,
        in_specs=(P("row", "col"), P(), P()),
        out_specs=P("row", "layer", "col"),
        check_vma=False,
    )
```

```python
import functools

import jax
import jax.numpy as jnp
from jax import lax
from jax.experimental import pallas as pl
from jax.experimental.pallas import tpu as pltpu
from jax.sharding import PartitionSpec as P

B = 128
TILE = 2
VMEM = 62 * 2**20


def swap(x, axis, distance):
    size = lax.axis_size(axis)
    return lax.ppermute(x, axis, [(i, i ^ distance) for i in range(size)])


def after(x, *earlier):
    return lax.optimization_barrier((x, *earlier))[0]


class Exchange:
    def __init__(self, own, whole, *gate):
        self.own, self.whole = [own], whole
        if gate:
            own = after(own, *gate)
        half = own.shape[0] // 2
        self.top, self.bottom = own[:half], own[half:]
        if whole:
            self.across, self.along = [swap(own, "row", 1)], [swap(own, "row", 2)]
            self.hops = self.across[0][:half], self.along[0][half:]
        else:
            self.hops = swap(self.top, "row", 1), swap(self.bottom, "row", 2)

    def second(self, *gate):
        if not self.whole:
            top, bottom = after(self.top, *gate), after(self.bottom, *gate)
            self.across = [self.hops[0], swap(bottom, "row", 1)]
            self.along = [swap(top, "row", 2), self.hops[1]]

    def relay(self, *gate):
        top, bottom = (after(x, *gate) if gate else x for x in self.hops)
        self.far = [swap(top, "row", 2), swap(bottom, "row", 1)]

    def near(self):
        return [(0, self.own), (1, self.across), (2, self.along)]

    def early(self):
        return [(0, self.own), (1, [self.hops[0], None]), (2, [None, self.hops[1]])]

    def late(self):
        return [(1, [None, self.across[1]]), (2, [self.along[0], None])]


def pick_kernel(start, where, keep, *refs):
    *columns, o_ref = refs
    i = pl.program_id(0)
    step = o_ref.shape[0] // B
    for q, x_ref in enumerate(columns):
        for t in range(step):
            kept = keep[i * step + t, start + q] != 0
            block = x_ref[pl.ds(t * B, B), :]
            o_ref[pl.ds(t * B, B), pl.ds(q * B, B)] = jnp.where(kept, block, jnp.zeros_like(block))


def pick_columns(density, keep, layer, layers, start, group):
    rows = density.shape[0]
    tile = 2 * TILE * B

    def column(q):
        return pl.BlockSpec((tile, B), lambda i, where, keep: (i, (start + q) * layers + where[0]))

    return pl.pallas_call(
        functools.partial(pick_kernel, start),
        grid_spec=pltpu.PrefetchScalarGridSpec(
            num_scalar_prefetch=2,
            grid=(rows // tile,),
            in_specs=[column(q) for q in range(group)],
            out_specs=pl.BlockSpec((tile, group * B), lambda i, *_: (i, 0)),
        ),
        out_shape=jax.ShapeDtypeStruct((rows, group * B), density.dtype),
        compiler_params=pltpu.CompilerParams(vmem_limit_bytes=VMEM),
        name="pick_columns",
    )(jnp.reshape(layer, (1,)), keep, *[density] * group)


def product_kernel(plan, full, scale, meta, *refs):
    refs = list(refs)
    take = lambda n: [refs.pop(0) for _ in range(n)]
    n_slot = meta.shape[0] // 4
    lhs, masks = take(n_slot), take(n_slot)
    panels = [(m, at, take(1)[0]) for m, at in plan]
    base = take(1)[0] if scale else None
    total, held, sems = refs[-3:]
    outs = refs[:-3]
    i = pl.program_id(0)
    tile = total.shape[0]
    depth = held.shape[0] // n_slot

    @pl.when(i == 0)
    def _():
        copies = []
        for m, start, panel in panels:
            at = pl.multiple_of(meta[m] * depth + start, B)
            copies.append(pltpu.make_async_copy(
                panel, held.at[pl.ds(at, panel.shape[0])], sems.at[len(copies)]))
        for copy in copies:
            copy.start()
        for copy in copies:
            copy.wait()

    total[...] = jnp.zeros_like(total)
    whole = all(panel.shape[0] == depth for _, _, panel in panels)
    step = depth if full or whole else depth // 2
    for s in range(n_slot):
        for at in range(0, depth, step):
            def add():
                kept = [
                    jnp.broadcast_to(masks[s][0, t:t + 1, at:at + step], (B, step))
                    for t in range(tile // B)
                ]
                kept = jnp.concatenate(kept, axis=0).astype(jnp.bfloat16)
                total[...] += jnp.dot(
                    lhs[s][:, at:at + step] * kept, held[pl.ds(s * depth + at, step), :],
                    preferred_element_type=jnp.float32)

            if full:
                add()
            else:
                pl.when(meta[2 * n_slot + 2 * s + at // (depth // 2)] != 0)(add)
    if scale:
        outs[0][...] = scale * base[...] - 2.0 * total[...]
        return
    outs[0][...] = total[...]
    if len(outs) > 1:
        outs[1][...] = total[...].astype(jnp.bfloat16)


def far_kernel(column, meta, keep, first_ref, second_ref, mask, top, bottom, total_in, *outs):
    if column is not None:
        outs = outs[-1:]
    i = pl.program_id(0)
    tile, width = total_in.shape
    half = top.shape[0]

    def run(x_ref):
        kept = [jnp.broadcast_to(mask[0, t:t + 1, :], (B, 2 * half)) for t in range(tile // B)]
        x = x_ref[...] * jnp.concatenate(kept, axis=0).astype(jnp.bfloat16)
        part = jnp.dot(x[:, :half], top[...], preferred_element_type=jnp.float32)
        part = part + jnp.dot(x[:, half:], bottom[...], preferred_element_type=jnp.float32)
        if column is None:
            total = total_in[...] + part
            outs[0][...] = total
            outs[1][...] = total.astype(jnp.bfloat16)
            return
        value = total_in[...] - 2.0 * part
        for t in range(tile // B):
            for q in range(width // B):
                kept = keep[i * (tile // B) + t, column * (width // B) + q] != 0
                block = value[t * B:(t + 1) * B, q * B:(q + 1) * B]
                outs[0][pl.ds(t * B, B), pl.ds(q * B, B)] = (
                    jnp.where(kept, block, 0.0).astype(outs[0].dtype))

    pl.when(meta[0] == 0)(lambda: run(first_ref))
    pl.when(meta[0] == 1)(lambda: run(second_ref))


def far_product(slots, owners, keep, sources, mask, panels, total, out=None, column=None):
    rows, width = total.shape
    tile, depth = TILE * B, rows
    n_slot = len(slots)
    per_source = n_slot // len(sources)
    slot = slots[-1]
    owner = sum(jnp.where(slot == s, owners[s], 0) for s in range(n_slot))
    meta = jnp.stack([slot // per_source, slot % per_source, owner])
    if len(sources) == 1:
        sources = [sources[0], sources[0]]

    def rows_of(h):
        def index(i, meta, keep):
            here = meta[0] == h
            return jnp.where(here, i, 0), jnp.where(here, meta[1], 0)
        return pl.BlockSpec((tile, depth), index)

    panel = pl.BlockSpec(panels[0].shape, lambda i, *_: (0, 0), pipeline_mode=pl.Buffered(1))
    row_block = pl.BlockSpec((tile, width), lambda i, *_: (i, 0))
    specs = [
        rows_of(0), rows_of(1),
        pl.BlockSpec((1, TILE, depth), lambda i, meta, keep: (i, 0, meta[2])),
        panel, panel, row_block,
    ]
    args = [*sources, mask, *panels, total]
    aliases = {}
    if column is None:
        out_shape = [jax.ShapeDtypeStruct((rows, width), t) for t in (jnp.float32, jnp.bfloat16)]
        out_specs = [row_block, row_block]
    else:
        if column > 0:
            specs.append(pl.BlockSpec(memory_space=pl.ANY))
            args.append(out)
            aliases = {2 + len(args) - 1: 0}
        out_shape = [jax.ShapeDtypeStruct(out if column == 0 else out.shape, jnp.bfloat16)]
        out_specs = [pl.BlockSpec((tile, width), lambda i, *_: (i, column))]
    result = pl.pallas_call(
        functools.partial(far_kernel, column),
        grid_spec=pltpu.PrefetchScalarGridSpec(
            num_scalar_prefetch=2, grid=(rows // tile,), in_specs=specs, out_specs=out_specs),
        out_shape=out_shape,
        input_output_aliases=aliases,
        cost_estimate=pl.CostEstimate(
            flops=2 * rows * depth * width, bytes_accessed=2 * rows * depth, transcendentals=0),
        compiler_params=pltpu.CompilerParams(vmem_limit_bytes=VMEM),
        name="far_product",
    )(meta, keep, *args)
    return result if column is None else result[0]


def product(panels, slots, owners, sources, mask, rounded=False, base=None, scale=None):
    rows = sources[0].shape[0]
    width = next(x for x in panels[0][1] if x is not None).shape[1]
    plan, arrays, covers = [], [], []
    for m, pieces in panels:
        for h, x in enumerate(pieces):
            if x is not None:
                start = h * (rows // len(pieces))
                plan.append((m, start))
                arrays.append(x)
                covers += [(m, k) for k in range(2) if start <= k * (rows // 2) < start + x.shape[0]]
    tile = TILE * B
    depth = rows
    steps = rows // tile
    n_slot = len(slots)
    per_source = n_slot // len(sources)
    full = len(covers) == 2 * n_slot
    used = [
        sum(((slots[m] == s).astype(jnp.int32) for m, k in covers if k == h), jnp.int32(0))
        for s in range(n_slot) for h in range(2)
    ]
    meta = jnp.stack([*slots, *owners, *used])
    specs, args = [], []
    for s in range(n_slot):
        def index(i, meta, s=s):
            here = meta[2 * n_slot + 2 * s] + meta[2 * n_slot + 2 * s + 1] != 0
            return i if full else jnp.where(here, i, 0), s % per_source
        specs.append(pl.BlockSpec((tile, depth), index))
        args.append(sources[s // per_source])
    for s in range(n_slot):
        specs.append(
            pl.BlockSpec((1, TILE, depth), lambda i, meta, s=s: (i, 0, meta[n_slot + s])))
        args.append(mask)
    specs += [pl.BlockSpec(memory_space=pl.ANY)] * len(arrays)
    args += arrays
    row_block = pl.BlockSpec((tile, width), lambda i, *_: (i, 0))
    if base is not None:
        specs.append(row_block)
        args.append(base)
    out_shape = [jax.ShapeDtypeStruct((rows, width), jnp.float32)]
    out_specs = [row_block]
    if rounded:
        out_shape.append(jax.ShapeDtypeStruct((rows, width), jnp.bfloat16))
        out_specs.append(row_block)
    flops = rows * depth * len(covers) * width
    result = pl.pallas_call(
        functools.partial(product_kernel, plan, full, scale),
        grid_spec=pltpu.PrefetchScalarGridSpec(
            num_scalar_prefetch=1,
            grid=(steps,),
            in_specs=specs,
            out_specs=out_specs,
            scratch_shapes=[
                pltpu.VMEM((tile, width), jnp.float32),
                pltpu.VMEM((n_slot * depth, width), jnp.bfloat16),
                pltpu.SemaphoreType.DMA((len(arrays),)),
            ],
        ),
        out_shape=out_shape,
        cost_estimate=pl.CostEstimate(
            flops=flops, bytes_accessed=rows * depth * len(covers), transcendentals=0),
        compiler_params=pltpu.CompilerParams(vmem_limit_bytes=VMEM),
        name="product",
    )(meta, *args)
    return result if rounded else result[0]


def shards(density, density_pattern, result_pattern):
    rows, cols = density.shape
    layers = lax.axis_size("layer")
    n_col = lax.axis_size("col")
    block_rows, block_cols = rows // B, cols // B
    group = block_cols // layers
    width = group * B
    r, c, l = (lax.axis_index(a) for a in ("row", "col", "layer"))
    n_chunk = 2 if group % 4 == 0 else 1
    chunk_w = width // n_chunk

    def pattern_tile(pattern):
        here = lax.dynamic_slice(pattern, (r * block_rows, c * block_cols), (block_rows, block_cols))
        return lax.dynamic_index_in_dim(here.reshape(block_rows, group, layers), l, 2, keepdims=False)

    if n_col == 2:
        sources = [density, swap(density, "col", 1)]
    else:
        sources = [lax.all_gather(density, "col", axis=1, tiled=True)]
    own_mask = pattern_tile(density_pattern)
    step = group // n_chunk
    own_chunks = [
        pick_columns(density, own_mask, l, layers, j * step, step) for j in range(n_chunk)
    ]
    row_mask = lax.dynamic_slice_in_dim(density_pattern, r * block_rows, block_rows, 0)
    n_block = row_mask.shape[1]
    mask = jnp.repeat(row_mask.astype(jnp.float32), B, axis=1)
    mask = mask.reshape(block_rows // TILE, TILE, n_block * B)
    keep = pattern_tile(result_pattern)
    n_slot = n_block * B // rows
    per_source = n_slot // len(sources)
    slots, owners = [], []
    for m in range(n_slot):
        owner = r ^ m
        source = (owner // per_source != c).astype(jnp.int32) if len(sources) == 2 else 0
        slots.append(source * per_source + owner % per_source)
        source = m // per_source
        owners.append((c ^ source) * per_source + m % per_source if len(sources) == 2 else jnp.int32(m))
    common = dict(slots=slots, owners=owners, sources=sources, mask=mask)
    run = functools.partial(product, **common)
    run_far = functools.partial(far_product, keep=keep, **common)

    def exchange(own, early=(), **how):
        first = Exchange(own[0], True)
        rest = [Exchange(x, False) for x in own[1:]]
        first.relay(*early)
        first.own = [after(own[0], *first.hops)]
        total = run(first.near(), **how)
        for x in rest:
            x.second(total)
        return first, rest, total

    first, rest, total = exchange(own_chunks, sources[1:])
    for x in rest:
        x.relay(total)
    sums = [run_far(panels=first.far, total=total)]
    sums += [run([*x.near(), (n_slot - 1, x.far)], rounded=True) for x in rest]
    squares = [square for square, _ in sums]
    first, rest, total = exchange([low for _, low in sums], base=squares[0], scale=3.0)
    totals = [run(x.early(), base=y, scale=3.0) for x, y in zip(rest, squares[1:])]
    for x, y in zip(rest, totals):
        x.relay(y)
    out = run_far(panels=first.far, total=total, out=(rows, width), column=0)
    for j, x in enumerate(rest, 1):
        total = run(x.late(), base=totals[j - 1], scale=1.0)
        out = run_far(panels=x.far, total=total, out=out, column=j)
    return out.reshape(rows, 1, width)


def solution(mesh):
    return jax.shard_map(
        shards,
        mesh=mesh,
        in_specs=(P("row", "col"), P(), P()),
        out_specs=P("row", "layer", "col"),
        check_vma=False,
    )
```

```python
import functools

import jax
import jax.numpy as jnp
from jax import lax
from jax.experimental import pallas as pl
from jax.experimental.pallas import tpu as pltpu
from jax.sharding import PartitionSpec as P

B = 128
TILE = 2
VMEM = 62 * 2**20


def swap(x, axis, distance):
    size = lax.axis_size(axis)
    return lax.ppermute(x, axis, [(i, i ^ distance) for i in range(size)])


def after(x, *earlier):
    return lax.optimization_barrier((x, *earlier))[0]


class Exchange:
    def __init__(self, own, whole, *gate):
        self.own, self.whole = [own], whole
        if gate:
            own = after(own, *gate)
        half = own.shape[0] // 2
        self.top, self.bottom = own[:half], own[half:]
        if whole:
            self.across, self.along = [swap(own, "row", 1)], [swap(own, "row", 2)]
            self.hops = self.across[0][:half], self.along[0][half:]
        else:
            self.hops = swap(self.top, "row", 1), swap(self.bottom, "row", 2)

    def second(self, *gate):
        if not self.whole:
            top, bottom = after(self.top, *gate), after(self.bottom, *gate)
            self.across = [self.hops[0], swap(bottom, "row", 1)]
            self.along = [swap(top, "row", 2), self.hops[1]]

    def relay(self, *gate):
        top, bottom = (after(x, *gate) if gate else x for x in self.hops)
        self.far = [swap(top, "row", 2), swap(bottom, "row", 1)]

    def near(self):
        return [(0, self.own), (1, self.across), (2, self.along)]

    def early(self):
        return [(0, self.own), (1, [self.hops[0], None]), (2, [None, self.hops[1]])]

    def late(self):
        return [(1, [None, self.across[1]]), (2, [self.along[0], None])]


def pick_kernel(start, where, keep, *refs):
    *columns, o_ref = refs
    i = pl.program_id(0)
    step = o_ref.shape[0] // B
    for q, x_ref in enumerate(columns):
        for t in range(step):
            kept = keep[i * step + t, start + q] != 0
            block = x_ref[pl.ds(t * B, B), :]
            o_ref[pl.ds(t * B, B), pl.ds(q * B, B)] = jnp.where(kept, block, jnp.zeros_like(block))


def pick_columns(density, keep, layer, layers, start, group):
    rows = density.shape[0]
    tile = 2 * TILE * B

    def column(q):
        return pl.BlockSpec((tile, B), lambda i, where, keep: (i, (start + q) * layers + where[0]))

    return pl.pallas_call(
        functools.partial(pick_kernel, start),
        grid_spec=pltpu.PrefetchScalarGridSpec(
            num_scalar_prefetch=2,
            grid=(rows // tile,),
            in_specs=[column(q) for q in range(group)],
            out_specs=pl.BlockSpec((tile, group * B), lambda i, *_: (i, 0)),
        ),
        out_shape=jax.ShapeDtypeStruct((rows, group * B), density.dtype),
        compiler_params=pltpu.CompilerParams(vmem_limit_bytes=VMEM),
        name="pick_columns",
    )(jnp.reshape(layer, (1,)), keep, *[density] * group)


def product_kernel(plan, full, scale, meta, *refs):
    refs = list(refs)
    take = lambda n: [refs.pop(0) for _ in range(n)]
    n_slot = meta.shape[0] // 4
    lhs, masks = take(n_slot), take(n_slot)
    panels = [(m, at, take(1)[0]) for m, at in plan]
    base = take(1)[0] if scale else None
    total, held, sems = refs[-3:]
    outs = refs[:-3]
    i = pl.program_id(0)
    tile = total.shape[0]
    depth = held.shape[0] // n_slot

    @pl.when(i == 0)
    def _():
        copies = []
        for m, start, panel in panels:
            at = pl.multiple_of(meta[m] * depth + start, B)
            copies.append(pltpu.make_async_copy(
                panel, held.at[pl.ds(at, panel.shape[0])], sems.at[len(copies)]))
        for copy in copies:
            copy.start()
        for copy in copies:
            copy.wait()

    total[...] = jnp.zeros_like(total)
    whole = all(panel.shape[0] == depth for _, _, panel in panels)
    step = depth if full or whole else depth // 2
    for s in range(n_slot):
        for at in range(0, depth, step):
            def add():
                kept = [
                    jnp.broadcast_to(masks[s][0, t:t + 1, at:at + step], (B, step))
                    for t in range(tile // B)
                ]
                kept = jnp.concatenate(kept, axis=0).astype(jnp.bfloat16)
                total[...] += jnp.dot(
                    lhs[s][:, at:at + step] * kept, held[pl.ds(s * depth + at, step), :],
                    preferred_element_type=jnp.float32)

            if full:
                add()
            else:
                pl.when(meta[2 * n_slot + 2 * s + at // (depth // 2)] != 0)(add)
    if scale:
        outs[0][...] = scale * base[...] - 2.0 * total[...]
        return
    outs[0][...] = total[...]
    if len(outs) > 1:
        outs[1][...] = total[...].astype(jnp.bfloat16)


def far_kernel(column, meta, keep, first_ref, second_ref, mask, top, bottom, total_in, *outs):
    if column is not None:
        outs = outs[-1:]
    i = pl.program_id(0)
    tile, width = total_in.shape
    half = top.shape[0]

    def run(x_ref):
        kept = [jnp.broadcast_to(mask[0, t:t + 1, :], (B, 2 * half)) for t in range(tile // B)]
        x = x_ref[...] * jnp.concatenate(kept, axis=0).astype(jnp.bfloat16)
        part = jnp.dot(x[:, :half], top[...], preferred_element_type=jnp.float32)
        part = part + jnp.dot(x[:, half:], bottom[...], preferred_element_type=jnp.float32)
        if column is None:
            total = total_in[...] + part
            outs[0][...] = total
            outs[1][...] = total.astype(jnp.bfloat16)
            return
        value = total_in[...] - 2.0 * part
        for t in range(tile // B):
            for q in range(width // B):
                kept = keep[i * (tile // B) + t, column * (width // B) + q] != 0
                block = value[t * B:(t + 1) * B, q * B:(q + 1) * B]
                outs[0][pl.ds(t * B, B), pl.ds(q * B, B)] = (
                    jnp.where(kept, block, 0.0).astype(outs[0].dtype))

    pl.when(meta[0] == 0)(lambda: run(first_ref))
    pl.when(meta[0] == 1)(lambda: run(second_ref))


def far_product(slots, owners, keep, sources, mask, panels, total, out=None, column=None):
    rows, width = total.shape
    tile, depth = 2 * TILE * B, rows
    mask = mask.reshape(rows // tile, 2 * TILE, mask.shape[2])
    n_slot = len(slots)
    per_source = n_slot // len(sources)
    slot = slots[-1]
    owner = sum(jnp.where(slot == s, owners[s], 0) for s in range(n_slot))
    meta = jnp.stack([slot // per_source, slot % per_source, owner])
    if len(sources) == 1:
        sources = [sources[0], sources[0]]

    def rows_of(h):
        def index(i, meta, keep):
            here = meta[0] == h
            return jnp.where(here, i, 0), jnp.where(here, meta[1], 0)
        return pl.BlockSpec((tile, depth), index)

    panel = pl.BlockSpec(panels[0].shape, lambda i, *_: (0, 0), pipeline_mode=pl.Buffered(1))
    row_block = pl.BlockSpec((tile, width), lambda i, *_: (i, 0))
    specs = [
        rows_of(0), rows_of(1),
        pl.BlockSpec((1, 2 * TILE, depth), lambda i, meta, keep: (i, 0, meta[2])),
        panel, panel, row_block,
    ]
    args = [*sources, mask, *panels, total]
    aliases = {}
    if column is None:
        out_shape = [jax.ShapeDtypeStruct((rows, width), t) for t in (jnp.float32, jnp.bfloat16)]
        out_specs = [row_block, row_block]
    else:
        if column > 0:
            specs.append(pl.BlockSpec(memory_space=pl.ANY))
            args.append(out)
            aliases = {2 + len(args) - 1: 0}
        out_shape = [jax.ShapeDtypeStruct(out if column == 0 else out.shape, jnp.bfloat16)]
        out_specs = [pl.BlockSpec((tile, width), lambda i, *_: (i, column))]
    result = pl.pallas_call(
        functools.partial(far_kernel, column),
        grid_spec=pltpu.PrefetchScalarGridSpec(
            num_scalar_prefetch=2, grid=(rows // tile,), in_specs=specs, out_specs=out_specs),
        out_shape=out_shape,
        input_output_aliases=aliases,
        cost_estimate=pl.CostEstimate(
            flops=2 * rows * depth * width, bytes_accessed=2 * rows * depth, transcendentals=0),
        compiler_params=pltpu.CompilerParams(vmem_limit_bytes=VMEM),
        name="far_product",
    )(meta, keep, *args)
    return result if column is None else result[0]


def product(panels, slots, owners, sources, mask, rounded=False, base=None, scale=None):
    rows = sources[0].shape[0]
    width = next(x for x in panels[0][1] if x is not None).shape[1]
    plan, arrays, covers = [], [], []
    for m, pieces in panels:
        for h, x in enumerate(pieces):
            if x is not None:
                start = h * (rows // len(pieces))
                plan.append((m, start))
                arrays.append(x)
                covers += [(m, k) for k in range(2) if start <= k * (rows // 2) < start + x.shape[0]]
    tile = TILE * B
    depth = rows
    steps = rows // tile
    n_slot = len(slots)
    per_source = n_slot // len(sources)
    full = len(covers) == 2 * n_slot
    used = [
        sum(((slots[m] == s).astype(jnp.int32) for m, k in covers if k == h), jnp.int32(0))
        for s in range(n_slot) for h in range(2)
    ]
    meta = jnp.stack([*slots, *owners, *used])
    specs, args = [], []
    for s in range(n_slot):
        def index(i, meta, s=s):
            here = meta[2 * n_slot + 2 * s] + meta[2 * n_slot + 2 * s + 1] != 0
            return i if full else jnp.where(here, i, 0), s % per_source
        specs.append(pl.BlockSpec((tile, depth), index))
        args.append(sources[s // per_source])
    for s in range(n_slot):
        specs.append(
            pl.BlockSpec((1, TILE, depth), lambda i, meta, s=s: (i, 0, meta[n_slot + s])))
        args.append(mask)
    specs += [pl.BlockSpec(memory_space=pl.ANY)] * len(arrays)
    args += arrays
    row_block = pl.BlockSpec((tile, width), lambda i, *_: (i, 0))
    if base is not None:
        specs.append(row_block)
        args.append(base)
    out_shape = [jax.ShapeDtypeStruct((rows, width), jnp.float32)]
    out_specs = [row_block]
    if rounded:
        out_shape.append(jax.ShapeDtypeStruct((rows, width), jnp.bfloat16))
        out_specs.append(row_block)
    flops = rows * depth * len(covers) * width
    result = pl.pallas_call(
        functools.partial(product_kernel, plan, full, scale),
        grid_spec=pltpu.PrefetchScalarGridSpec(
            num_scalar_prefetch=1,
            grid=(steps,),
            in_specs=specs,
            out_specs=out_specs,
            scratch_shapes=[
                pltpu.VMEM((tile, width), jnp.float32),
                pltpu.VMEM((n_slot * depth, width), jnp.bfloat16),
                pltpu.SemaphoreType.DMA((len(arrays),)),
            ],
        ),
        out_shape=out_shape,
        cost_estimate=pl.CostEstimate(
            flops=flops, bytes_accessed=rows * depth * len(covers), transcendentals=0),
        compiler_params=pltpu.CompilerParams(vmem_limit_bytes=VMEM),
        name="product",
    )(meta, *args)
    return result if rounded else result[0]


def shards(density, density_pattern, result_pattern):
    rows, cols = density.shape
    layers = lax.axis_size("layer")
    n_col = lax.axis_size("col")
    block_rows, block_cols = rows // B, cols // B
    group = block_cols // layers
    width = group * B
    r, c, l = (lax.axis_index(a) for a in ("row", "col", "layer"))
    n_chunk = 2 if group % 4 == 0 else 1
    chunk_w = width // n_chunk

    def pattern_tile(pattern):
        here = lax.dynamic_slice(pattern, (r * block_rows, c * block_cols), (block_rows, block_cols))
        return lax.dynamic_index_in_dim(here.reshape(block_rows, group, layers), l, 2, keepdims=False)

    if n_col == 2:
        sources = [density, swap(density, "col", 1)]
    else:
        sources = [lax.all_gather(density, "col", axis=1, tiled=True)]
    own_mask = pattern_tile(density_pattern)
    step = group // n_chunk
    own_chunks = [
        pick_columns(density, own_mask, l, layers, j * step, step) for j in range(n_chunk)
    ]
    row_mask = lax.dynamic_slice_in_dim(density_pattern, r * block_rows, block_rows, 0)
    n_block = row_mask.shape[1]
    mask = jnp.repeat(row_mask.astype(jnp.float32), B, axis=1)
    mask = mask.reshape(block_rows // TILE, TILE, n_block * B)
    keep = pattern_tile(result_pattern)
    n_slot = n_block * B // rows
    per_source = n_slot // len(sources)
    slots, owners = [], []
    for m in range(n_slot):
        owner = r ^ m
        source = (owner // per_source != c).astype(jnp.int32) if len(sources) == 2 else 0
        slots.append(source * per_source + owner % per_source)
        source = m // per_source
        owners.append((c ^ source) * per_source + m % per_source if len(sources) == 2 else jnp.int32(m))
    common = dict(slots=slots, owners=owners, sources=sources, mask=mask)
    run = functools.partial(product, **common)
    run_far = functools.partial(far_product, keep=keep, **common)

    def exchange(own, early=(), **how):
        first = Exchange(own[0], True)
        rest = [Exchange(x, False) for x in own[1:]]
        first.relay(*early)
        first.own = [after(own[0], *first.hops)]
        total = run(first.near(), **how)
        for x in rest:
            x.second(total)
        return first, rest, total

    first, rest, total = exchange(own_chunks, sources[1:])
    for x in rest:
        x.relay(total)
    sums = [run_far(panels=first.far, total=total)]
    sums += [run([*x.near(), (n_slot - 1, x.far)], rounded=True) for x in rest]
    squares = [square for square, _ in sums]
    first, rest, total = exchange([low for _, low in sums], base=squares[0], scale=3.0)
    totals = [run(x.early(), base=y, scale=3.0) for x, y in zip(rest, squares[1:])]
    for x, y in zip(rest, totals):
        x.relay(y)
    out = run_far(panels=first.far, total=total, out=(rows, width), column=0)
    for j, x in enumerate(rest, 1):
        total = run(x.late(), base=totals[j - 1], scale=1.0)
        out = run_far(panels=x.far, total=total, out=out, column=j)
    return out.reshape(rows, 1, width)


def solution(mesh):
    return jax.shard_map(
        shards,
        mesh=mesh,
        in_specs=(P("row", "col"), P(), P()),
        out_specs=P("row", "layer", "col"),
        check_vma=False,
    )
```
